32 devices in a mesh: groups: 2 (over x), terms: 16 (over z, y, core).
Axes of the slice: x: 2, y: 2, z: 4, core: 2. Of those that a mesh axis runs over, the one named last changes fastest.
Arguments:
- psi: bfloat16 [32768, 384], P(('groups', 'terms')), parts along dimension 0, may hold values from -6 to 6
- left_env: bfloat16 [32, 16384, 128], P('groups', 'terms'), parts along dimension 0, may hold values from -0.125 to 0.125
- right_env: bfloat16 [524288, 128], P(('groups', 'terms')), parts along dimension 0, may hold values from -0.5 to 0.5
- target: int32 [32, 128], P('groups'), parts along dimension 0, may hold values from -1 to 127, as said below
Outputs:
- h_psi: bfloat16 [32768, 384], P(('groups', 'terms')), parts along dimension 0
The draws below stay inside these ranges and needn't reach their ends.
There are 2 independent parts, one for each index of `groups`. The reference program is written for one: setup_inputs(seed, part) draws one part's arguments, and reference() takes and returns one part's arrays. A program takes and returns all parts, laid end to end along the dimension named above; each array names one. Nothing has to cross between parts.
Inputs may be any that keep to these rules, and one draw needn't show every extreme that they name: Each term t has one shift q in -2..2, and target[t, c] = c + q where that lies in 0..127, else -1.
All inputs are finite; a program needn't handle non-finite values.
Results may differ from the reference program's by a relative error of at most 0.0058.
Values may be sent and summed in bfloat16 or wider, within the bound.
No kernel may reach another device: no remote copies, remote signals or barrier semaphores. Data moves between devices by JAX's collectives and lax.ppermute only.
A program may use at most 128 MiB of HBM per device.

```python
import jax
import jax.numpy as jnp
from jax import lax

DB = 128
TERMS = 16
VECTORS = 3
NB = 128
STRIDE = 1


def draw_target(key, part):
    key = jax.random.fold_in(key, 11)
    shifts = jax.random.randint(key, (TERMS,), -2, 3).astype(jnp.int32)
    shifts = shifts.at[0].set(1).at[1].set(0)
    landing = jnp.arange(NB, dtype=jnp.int32)[None, :] + shifts[:, None]
    inside = (landing >= 0) & (landing < NB)
    return jnp.where(inside, landing, -1).astype(jnp.int32)


def block_levels(key, shape, cuts, least, largest):
    gain, own = 1.0, jax.random.fold_in(key, 6)
    for axis_at, blocks in cuts:
        steps = jnp.exp(jax.random.uniform(jax.random.fold_in(own, axis_at), (blocks,), jnp.float32, least / len(cuts), largest / len(cuts)))
        gain = gain * jnp.repeat(steps, shape[axis_at] // blocks).reshape([-1 if axis == axis_at else 1 for axis in range(len(shape))])
    return gain


def noise(stream_key, extent, width, limit, cuts=(), kind=jnp.bfloat16):
    array = width * jax.random.normal(stream_key, extent, jnp.float32)
    if cuts:
        array = array * block_levels(stream_key, extent, cuts, -0.22, 0.18)
    return jnp.clip(array, -limit, limit).astype(kind)


def setup_inputs(seed: int = 0, part: int = 0) -> dict:
    arg_keys = jax.random.split(jax.random.key(seed), 5)
    own_keys = jax.random.split(jax.random.fold_in(arg_keys[4], part), 5)
    psi = noise(own_keys[0], (NB * DB, VECTORS * DB), 1.0, 6.0, ((0, 16),))
    left_env = noise(own_keys[1], (TERMS, NB * DB, DB), (DB * TERMS) ** -0.5, 0.125, ((1, 16),))
    right_env = noise(own_keys[2], (TERMS * NB * DB, DB), DB ** -0.5, 0.5, ((0, 16),))
    target = draw_target(jax.random.fold_in(jax.random.fold_in(arg_keys[4], part), 71), part)
    return {"psi": psi, "left_env": left_env, "right_env": right_env, "target": target}


def reference(psi, left_env, right_env, target):
    columns = VECTORS * DB
    blocks = psi.reshape(NB, DB, columns).astype(jnp.float32)
    left_all = left_env.reshape(TERMS, NB, DB, DB)
    right_all = right_env.reshape(TERMS, STRIDE, NB // STRIDE, DB, DB)
    right_all = jnp.transpose(right_all, (0, 2, 1, 3, 4)).reshape(TERMS, NB, DB, DB)

    def accumulate(summed, inputs):
        left_term, right_term, targets = inputs
        mixed = jnp.einsum("cab,cbk->cak", left_term.astype(jnp.float32), blocks)
        mixed = jnp.where((targets >= 0)[:, None, None], mixed, jnp.zeros_like(mixed)).astype(jnp.bfloat16)
        mixed = lax.optimization_barrier(mixed)
        mixed = mixed.reshape(NB, DB, VECTORS, DB).astype(jnp.float32)
        term_part = jnp.einsum("cavb,cbm->cavm", mixed, right_term.astype(jnp.float32)).astype(jnp.bfloat16)
        term_part = lax.optimization_barrier(term_part)
        term_part = term_part.reshape(NB, DB, columns).astype(jnp.float32)
        slot_ids = jnp.where(targets >= 0, targets, NB).astype(jnp.int32)
        return summed.at[slot_ids].add(term_part, mode="drop"), None

    summed = jnp.zeros((NB, DB, columns), jnp.float32)
    summed, unused = lax.scan(accumulate, summed, (left_all, right_all, target))
    return summed.reshape(NB * DB, columns).astype(jnp.bfloat16)
```

```python
import functools

import jax
import jax.numpy as jnp
from jax import lax
from jax.experimental import pallas as pl
from jax.experimental.pallas import tpu as pltpu
from jax.sharding import PartitionSpec as P

REACH = 2
ORDER = (8, 1, 13, 4, 10, 2, 15, 5, 9, 3, 12, 6, 7)
LAST = (11, 14)
GROUPS = ((0, 8, 1, 13), (4, 10, 2, 15), (5, 9, 3, 12), (6, 7))


def params(megabytes=40):
    return pltpu.CompilerParams(vmem_limit_bytes=megabytes * 2**20)


def spec(block, index):
    return pl.BlockSpec(block, index)


def cost(pairs, width, columns, extra_bytes=0):
    return pl.CostEstimate(
        flops=pairs * 2 * width * width * columns,
        bytes_accessed=pairs * width * (columns + width) * 2 + extra_bytes,
        transcendentals=0,
    )


def mix_kernel(places, me_ref, target_ref, left_ref, psi_ref, mixed_ref):
    for slot, block in enumerate(places):
        product = jnp.dot(left_ref[0, block], psi_ref[block], preferred_element_type=jnp.float32)
        mixed_ref[0, slot] = product.astype(mixed_ref.dtype)


def mix(me, target, left_env, psi, terms_of, places):
    terms, blocks, width, _ = left_env.shape
    columns = psi.shape[2]
    return pl.pallas_call(
        functools.partial(mix_kernel, places),
        grid_spec=pltpu.PrefetchScalarGridSpec(
            num_scalar_prefetch=2,
            grid=(terms,),
            in_specs=[
                spec((1, blocks, width, width), lambda s, me, target: (terms_of(me[0], s), 0, 0, 0)),
                spec((blocks, width, columns), lambda s, me, target: (0, 0, 0)),
            ],
            out_specs=spec((1, blocks, width, columns), lambda s, me, target: (s, 0, 0, 0)),
        ),
        out_shape=jax.ShapeDtypeStruct((terms, blocks, width, columns), jnp.bfloat16),
        cost_estimate=cost(terms * blocks, width, columns),
        compiler_params=params(),
        name="mix",
    )(me, target, left_env, psi)


def accumulate(acc, mixed, right, shift, slots, rows, base):
    width = right.shape[-1]
    columns = mixed.shape[-1]
    vectors = columns // width
    for slot, piece, row in zip(slots, range(len(slots)), rows):
        tall = jnp.concatenate(
            [mixed[0, slot, :, k * width : (k + 1) * width] for k in range(vectors)], axis=0
        )
        product = jnp.dot(tall, right[piece], preferred_element_type=jnp.float32)
        start = pl.multiple_of((row + base + shift) * width, width)
        for k in range(vectors):
            lanes = slice(k * width, (k + 1) * width)
            acc[pl.ds(start, width), lanes] += product[k * width : (k + 1) * width]


def shift_of(me_ref, target_ref, terms_of, s):
    return target_ref[terms_of(me_ref[0], s), REACH] - REACH


def group_kernel(patterns, terms_of, slots, rows, first, own, me_ref, target_ref, *refs):
    refs = list(refs)
    mixed = [refs.pop(0) for _ in patterns]
    right = [refs.pop(0) for _ in patterns]
    if first:
        (acc,) = refs
        acc[...] = jnp.zeros_like(acc)
    else:
        before, acc = refs
        acc[...] = before[...]
    for s, m, r in zip(patterns, mixed, right):
        accumulate(
            acc, m, r.at[0] if own and s == 0 else r, shift_of(me_ref, target_ref, terms_of, s), slots, rows, REACH
        )


def edge_kernel(patterns, terms_of, slots, rows, blocks, me_ref, target_ref, *refs):
    refs = list(refs)
    mixed = [refs.pop(0) for _ in patterns]
    right = [refs.pop(0) for _ in patterns]
    before, inner, to_left, to_right, acc = refs
    width = right[0].shape[-1]
    acc[...] = before[...]
    for s, m, r in zip(patterns, mixed, right):
        accumulate(acc, m, r, shift_of(me_ref, target_ref, terms_of, s), slots, rows, REACH)
    halo = REACH * width
    to_left[...] = acc[:halo].astype(to_left.dtype)
    to_right[...] = acc[halo + blocks * width :].astype(to_right.dtype)
    inner[...] = acc[halo : halo + blocks * width]


def last_kernel(patterns, terms_of, slots, rows, me_ref, target_ref, *refs):
    refs = list(refs)
    mixed = [refs.pop(0) for _ in patterns]
    right = [refs.pop(0) for _ in patterns]
    before, from_left, from_right, out, acc = refs
    halo = from_left.shape[0]
    acc[...] = before[...]
    acc[:halo] += from_left[...].astype(jnp.float32)
    acc[-halo:] += from_right[...].astype(jnp.float32)
    for s, m, r in zip(patterns, mixed, right):
        accumulate(acc, m, r, shift_of(me_ref, target_ref, terms_of, s), slots, rows, 0)
    out[...] = acc[...].astype(out.dtype)


def whole_spec(x):
    return spec(x.shape, lambda i, me, target, nd=x.ndim: (0,) * nd)


def shards(psi, left_env, right_env, target):
    terms = target.shape[0]
    width = left_env.shape[2]
    columns = psi.shape[1]
    devices = lax.axis_size("terms")
    stride = devices // terms
    blocks = psi.shape[0] // width
    per_class = blocks // stride
    me = lax.axis_index("terms")
    me_ref = me.astype(jnp.int32).reshape(1)
    edges = tuple(c for c in range(blocks) if c < REACH or c >= blocks - REACH)
    inside = tuple(c for c in range(blocks) if c not in edges)
    places = inside + edges
    slot_of = {c: i for i, c in enumerate(places)}
    by_partner = stride == 1 and terms == len(ORDER) + len(LAST) + 1
    terms_of = (lambda own, s: jnp.bitwise_xor(own, s)) if by_partner else (lambda own, s: s)

    psi_blocks = psi.reshape(blocks, width, columns)
    left_blocks = left_env.reshape(terms, blocks, width, width)

    def send(s, rows=None):
        right = right_env.reshape(devices, blocks, width, width)
        mine = lax.dynamic_index_in_dim(right, jnp.bitwise_xor(me, s), 0, keepdims=False)
        if rows is not None:
            mine = jnp.concatenate([mine[a:b] for a, b in rows], axis=0)
        return lax.ppermute(mine, "terms", [(i, i ^ s) for i in range(devices)])

    if by_partner:
        pieces = {s: send(s) for s in ORDER}
        edge_pieces = {s: send(s, ((0, REACH), (blocks - REACH, blocks))) for s in LAST}
        inner_pieces = {s: send(s, ((REACH, blocks - REACH),)) for s in LAST}
        pieces[0] = right_env.reshape(devices, blocks, width, width)
        groups, last = GROUPS, LAST
    else:
        sent = right_env.reshape(devices, per_class, width, width)
        got = lax.all_to_all(sent, "terms", split_axis=0, concat_axis=0, tiled=True)
        got = got.reshape(terms, stride, per_class, width, width)
        got = jnp.swapaxes(got, 1, 2).reshape(terms, blocks, width, width)
        last = (terms - 1,)
        pieces = {s: got[s] for s in range(terms - 1)}
        edge_pieces = {s: jnp.concatenate([got[s, :REACH], got[s, -REACH:]], axis=0) for s in last}
        inner_pieces = {s: got[s, REACH:-REACH] for s in last}
        groups = tuple(tuple(range(a, min(a + 4, terms - 1))) for a in range(0, terms - 1, 4))

    mixed = mix(me_ref, target, left_blocks, psi_blocks, terms_of, places)

    def mixed_spec(s, part, parts):
        count = len(part)
        at = slot_of[part[0]] // count if parts > 1 else 0
        return spec((1, count, width, columns), lambda i, me, target: (s, at, 0, 0))

    padded = (blocks + 2 * REACH) * width
    acc_shape = jax.ShapeDtypeStruct((padded, columns), jnp.float32)
    core_shape = jax.ShapeDtypeStruct((blocks * width, columns), jnp.float32)
    halo_shape = jax.ShapeDtypeStruct((REACH * width, columns), jnp.bfloat16)
    out_shape = jax.ShapeDtypeStruct((blocks * width, columns), jnp.bfloat16)
    everything = tuple(range(blocks))

    def call(kernel, patterns, specs, operands, outs, scratch, pairs, name):
        single = not isinstance(outs, tuple)
        out_list = (outs,) if single else outs
        out_specs = tuple(whole_spec(x) for x in out_list)
        return pl.pallas_call(
            kernel,
            grid_spec=pltpu.PrefetchScalarGridSpec(
                num_scalar_prefetch=2,
                grid=(1,),
                in_specs=specs,
                out_specs=out_specs[0] if single else out_specs,
                scratch_shapes=scratch,
            ),
            out_shape=outs,
            cost_estimate=cost(pairs, width, columns, 2 * padded * columns * 4),
            compiler_params=params(),
            name=name,
        )(me_ref, target, *operands)

    acc = None
    for number, patterns in enumerate(groups):
        specs = [mixed_spec(s, places, 1) for s in patterns]
        operands = [mixed for _ in patterns]
        for s in patterns:
            if by_partner and s == 0:
                specs.append(spec((1, blocks, width, width), lambda i, me, target: (me[0], 0, 0, 0)))
            else:
                specs.append(whole_spec(pieces[s]))
            operands.append(pieces[s])
        if number:
            specs.append(whole_spec(acc))
            operands.append(acc)
        kernel = functools.partial(
            group_kernel, patterns, terms_of, tuple(slot_of[c] for c in everything), everything, number == 0, by_partner
        )
        acc = call(kernel, patterns, specs, operands, acc_shape, (), len(patterns) * blocks, "add_terms")

    specs = [mixed_spec(s, edges, 2) for s in last] + [whole_spec(edge_pieces[s]) for s in last] + [whole_spec(acc)]
    operands = [mixed for _ in last] + [edge_pieces[s] for s in last] + [acc]
    kernel = functools.partial(edge_kernel, last, terms_of, tuple(range(len(edges))), edges, blocks)
    core, to_left, to_right = call(
        kernel, last, specs, operands, (core_shape, halo_shape, halo_shape),
        (pltpu.VMEM(acc_shape.shape, jnp.float32),), len(last) * len(edges), "add_edges",
    )
    from_right = lax.ppermute(to_left, "terms", [(i + 1, i) for i in range(devices - 1)])
    from_left = lax.ppermute(to_right, "terms", [(i, i + 1) for i in range(devices - 1)])

    specs = [mixed_spec(s, inside, 2) for s in last] + [whole_spec(inner_pieces[s]) for s in last]
    specs += [whole_spec(core), whole_spec(from_left), whole_spec(from_right)]
    operands = [mixed for _ in last] + [inner_pieces[s] for s in last] + [core, from_left, from_right]
    kernel = functools.partial(last_kernel, last, terms_of, tuple(range(len(inside))), inside)
    return call(
        kernel, last, specs, operands, out_shape,
        (pltpu.VMEM(core_shape.shape, jnp.float32),), len(last) * len(inside), "add_rest",
    )


def solution(mesh):
    return jax.shard_map(
        shards,
        mesh=mesh,
        in_specs=(
            P(("groups", "terms"), None),
            P("groups", "terms", None),
            P(("groups", "terms"), None),
            P("groups", None),
        ),
        out_specs=P(("groups", "terms"), None),
        check_vma=False,
    )
```

```python
import functools

import jax
import jax.numpy as jnp
from jax import lax
from jax.experimental import pallas as pl
from jax.experimental.pallas import tpu as pltpu
from jax.sharding import PartitionSpec as P

REACH = 2
FIRST = 8
EARLY = (12, 4)
LATE = (6, 2)
LAST = (10, 14)


def params(megabytes=40):
    return pltpu.CompilerParams(vmem_limit_bytes=megabytes * 2**20)


def after(x, *done):
    return lax.optimization_barrier((x, *done))[0]


def spec(block, index):
    return pl.BlockSpec(block, index)


def cost(pairs, width, columns, extra_bytes=0):
    return pl.CostEstimate(
        flops=pairs,
        bytes_accessed=pairs,
        transcendentals=0,
    )


def mix_kernel(places, me_ref, target_ref, left_ref, psi_ref, mixed_ref):
    for slot, block in enumerate(places):
        product = jnp.dot(left_ref[0, block], psi_ref[block], preferred_element_type=jnp.float32)
        mixed_ref[0, slot] = product.astype(mixed_ref.dtype)


def mix(me, target, left_env, psi, terms_of, places):
    terms, blocks, width, _ = left_env.shape
    columns = psi.shape[2]
    return pl.pallas_call(
        functools.partial(mix_kernel, places),
        grid_spec=pltpu.PrefetchScalarGridSpec(
            num_scalar_prefetch=2,
            grid=(terms,),
            in_specs=[
                spec((1, blocks, width, width), lambda s, me, target: (terms_of(me[0], s), 0, 0, 0)),
                spec((blocks, width, columns), lambda s, me, target: (0, 0, 0)),
            ],
            out_specs=spec((1, blocks, width, columns), lambda s, me, target: (s, 0, 0, 0)),
        ),
        out_shape=jax.ShapeDtypeStruct((terms, blocks, width, columns), jnp.bfloat16),
        cost_estimate=cost(terms * blocks, width, columns),
        compiler_params=params(),
        name="mix",
    )(me, target, left_env, psi)


def accumulate(acc, mixed, right, shift, slots, rows, base):
    width = right.shape[-1]
    columns = mixed.shape[-1]
    vectors = columns // width
    for slot, piece, row in zip(slots, range(len(slots)), rows):
        tall = jnp.concatenate(
            [mixed[0, slot, :, k * width : (k + 1) * width] for k in range(vectors)], axis=0
        )
        product = jnp.dot(tall, right[piece], preferred_element_type=jnp.float32)
        start = pl.multiple_of((row + base + shift) * width, width)
        for k in range(vectors):
            lanes = slice(k * width, (k + 1) * width)
            acc[pl.ds(start, width), lanes] += product[k * width : (k + 1) * width]


def shift_of(me_ref, target_ref, terms_of, s):
    return target_ref[terms_of(me_ref[0], s), REACH] - REACH


def group_kernel(patterns, terms_of, slots, rows, first, me_ref, target_ref, *refs):
    refs = list(refs)
    mixed = [refs.pop(0) for _ in patterns]
    right = [refs.pop(0) for _ in patterns]
    if first:
        (acc,) = refs
        acc[...] = jnp.zeros_like(acc)
    else:
        before, acc = refs
        acc[...] = before[...]
    for s, m, r in zip(patterns, mixed, right):
        accumulate(acc, m, r.at[0], shift_of(me_ref, target_ref, terms_of, s), slots, rows, REACH)


def edge_kernel(patterns, terms_of, slots, rows, blocks, me_ref, target_ref, *refs):
    refs = list(refs)
    mixed = [refs.pop(0) for _ in patterns]
    right = [refs.pop(0) for _ in patterns]
    before, inner, to_left, to_right, acc = refs
    width = right[0].shape[-1]
    acc[...] = before[...]
    for s, m, r in zip(patterns, mixed, right):
        accumulate(acc, m, r.at[0], shift_of(me_ref, target_ref, terms_of, s), slots, rows, REACH)
    halo = REACH * width
    to_left[...] = acc[:halo].astype(to_left.dtype)
    to_right[...] = acc[halo + blocks * width :].astype(to_right.dtype)
    inner[...] = acc[halo : halo + blocks * width]


def rest_kernel(patterns, terms_of, slots, rows, me_ref, target_ref, *refs):
    refs = list(refs)
    mixed = [refs.pop(0) for _ in patterns]
    right = [refs.pop(0) for _ in patterns]
    before, acc = refs
    acc[...] = before[...]
    for s, m, r in zip(patterns, mixed, right):
        accumulate(acc, m, r.at[0], shift_of(me_ref, target_ref, terms_of, s), slots, rows, 0)


def last_kernel(patterns, terms_of, slots, rows, me_ref, target_ref, *refs):
    refs = list(refs)
    mixed = [refs.pop(0) for _ in patterns]
    right = [refs.pop(0) for _ in patterns]
    before, from_left, from_right, out, acc = refs
    halo = from_left.shape[0]
    acc[...] = before[...]
    acc[:halo] += from_left[...].astype(jnp.float32)
    acc[-halo:] += from_right[...].astype(jnp.float32)
    for s, m, r in zip(patterns, mixed, right):
        accumulate(acc, m, r.at[0], shift_of(me_ref, target_ref, terms_of, s), slots, rows, 0)
    out[...] = acc[...].astype(out.dtype)


def whole_spec(x):
    return spec(x.shape, lambda i, me, target, nd=x.ndim: (0,) * nd)


def shards(psi, left_env, right_env, target):
    terms = target.shape[0]
    width = left_env.shape[2]
    columns = psi.shape[1]
    devices = lax.axis_size("terms")
    stride = devices // terms
    blocks = psi.shape[0] // width
    per_class = blocks // stride
    me = lax.axis_index("terms")
    me_ref = me.astype(jnp.int32).reshape(1)
    edges = tuple(c for c in range(blocks) if c < REACH or c >= blocks - REACH)
    inside = tuple(c for c in range(blocks) if c not in edges)
    places = inside + edges
    slot_of = {c: i for i, c in enumerate(places)}
    by_partner = stride == 1 and terms == 16
    terms_of = (lambda own, s: jnp.bitwise_xor(own, s)) if by_partner else (lambda own, s: s)

    psi_blocks = psi.reshape(blocks, width, columns)
    left_blocks = left_env.reshape(terms, blocks, width, width)

    right = right_env.reshape(devices, per_class, width, width)

    def move(operand, s):
        return lax.ppermute(operand, "terms", [(i, i ^ s) for i in range(devices)])

    def pick(source, index, start, count):
        return lax.dynamic_slice(source, (index, start, 0, 0), (1, count, width, width))

    def pair_message(source, exchanged, s, rows):
        partner = jnp.bitwise_xor(me, s)
        parts = [
            jnp.concatenate([pick(array, partner, a, b - a) for a, b in rows], axis=1)
            for array in (source, exchanged)
        ]
        return jnp.concatenate(parts, axis=0)

    def both(patterns):
        return tuple(p for s in patterns for p in (s, s + 1))

    def piece_spec(array, at):
        block = (1, *array.shape[1:])
        if callable(at):
            return spec(block, lambda i, me, target: (at(me[0]), 0, 0, 0))
        return spec(block, lambda i, me, target: (at, 0, 0, 0))

    def mixed_spec(s, part, parts):
        count = len(part)
        at = slot_of[part[0]] // count if parts > 1 else 0
        return spec((1, count, width, columns), lambda i, me, target: (s, at, 0, 0))

    padded = (blocks + 2 * REACH) * width
    acc_shape = jax.ShapeDtypeStruct((padded, columns), jnp.float32)
    core_shape = jax.ShapeDtypeStruct((blocks * width, columns), jnp.float32)
    halo_shape = jax.ShapeDtypeStruct((REACH * width, columns), jnp.bfloat16)
    out_shape = jax.ShapeDtypeStruct((blocks * width, columns), jnp.bfloat16)
    everything = tuple(range(blocks))

    def call(kernel, patterns, specs, operands, outs, scratch, pairs, name):
        single = not isinstance(outs, tuple)
        out_list = (outs,) if single else outs
        out_specs = tuple(whole_spec(x) for x in out_list)
        return pl.pallas_call(
            kernel,
            grid_spec=pltpu.PrefetchScalarGridSpec(
                num_scalar_prefetch=2,
                grid=(1,),
                in_specs=specs,
                out_specs=out_specs[0] if single else out_specs,
                scratch_shapes=scratch,
            ),
            out_shape=outs,
            cost_estimate=cost(pairs, width, columns, 2 * padded * columns * 4),
            compiler_params=params(),
            name=name,
        )(me_ref, target, *operands)

    def group(patterns, acc):
        specs = [mixed_spec(s, places, 1) for s in patterns]
        operands = [mixed for _ in patterns]
        for s in patterns:
            array, at = pieces[s]
            specs.append(piece_spec(array, at))
            operands.append(array)
        if acc is not None:
            specs.append(whole_spec(acc))
            operands.append(acc)
        kernel = functools.partial(
            group_kernel, patterns, terms_of, tuple(slot_of[c] for c in everything), everything, acc is None
        )
        return call(kernel, patterns, specs, operands, acc_shape, (), len(patterns) * blocks, "add_terms")

    if by_partner:
        everywhere = ((0, blocks),)
        outer = ((0, REACH), (blocks - REACH, blocks))
        inner = ((REACH, blocks - REACH),)
        exchanged = move(right, 1)
        first = pick(right, jnp.bitwise_xor(me, FIRST), 0, blocks)
        pieces = {0: (right, lambda own: own), 1: (exchanged, lambda own: own), FIRST: (move(first, FIRST), 0)}
        edge_pieces, inner_pieces = {}, {}

        def send(store, source, exchanged, s, rows):
            message = pair_message(source, exchanged, s, rows)
            got = move(message, s)
            store[s], store[s + 1] = (got, 0), (got, 1)
            return message

        source, relayed = after(right, first), exchanged
        messages = []
        for s in EARLY:
            messages.append(send(pieces, source, relayed, s, everywhere))
            source, relayed = after(right, messages[-1]), after(exchanged, messages[-1])
        messages.append(pick(relayed, jnp.bitwise_xor(me, FIRST), 0, blocks))
        pieces[FIRST + 1] = (move(messages[-1], FIRST), 0)
        mixed = mix(me_ref, target, after(left_blocks, *messages), psi_blocks, terms_of, places)
        source, relayed = after(right, mixed), after(exchanged, mixed)
        for s in LAST:
            send(edge_pieces, source, relayed, s, outer)
        for s in LATE:
            send(pieces, source, relayed, s, everywhere)
        acc = group((0, 1, FIRST) + both(EARLY), None)
        source, relayed = after(right, acc), after(exchanged, acc)
        for s in LAST:
            send(inner_pieces, source, relayed, s, inner)
        acc = group((FIRST + 1,) + both(LATE), acc)
        last = both(LAST)
    else:
        got = lax.all_to_all(right, "terms", split_axis=0, concat_axis=0, tiled=True)
        got = got.reshape(terms, stride, per_class, width, width)
        got = jnp.swapaxes(got, 1, 2).reshape(terms, blocks, width, width)
        mixed = mix(me_ref, target, left_blocks, psi_blocks, terms_of, places)
        last = (terms - 1,)
        pieces = {s: (got, s) for s in range(terms - 1)}
        edge_pieces = {s: (jnp.concatenate([got[s:, :REACH], got[s:, -REACH:]], axis=1), 0) for s in last}
        inner_pieces = {s: (got[s:, REACH:-REACH], 0) for s in last}
        acc = None
        for a in range(0, terms - 1, 4):
            acc = group(tuple(range(a, min(a + 4, terms - 1))), acc)

    specs = [mixed_spec(s, edges, 2) for s in last] + [piece_spec(*edge_pieces[s]) for s in last] + [whole_spec(acc)]
    operands = [mixed for _ in last] + [edge_pieces[s][0] for s in last] + [acc]
    kernel = functools.partial(edge_kernel, last, terms_of, tuple(range(len(edges))), edges, blocks)
    core, to_left, to_right = call(
        kernel, last, specs, operands, (core_shape, halo_shape, halo_shape),
        (pltpu.VMEM(acc_shape.shape, jnp.float32),), len(last) * len(edges), "add_edges",
    )
    from_right = lax.ppermute(to_left, "terms", [(i + 1, i) for i in range(devices - 1)])
    from_left = lax.ppermute(to_right, "terms", [(i, i + 1) for i in range(devices - 1)])

    def rest(kernel, patterns, extra, out, scratch):
        specs = [mixed_spec(s, inside, 2) for s in patterns] + [piece_spec(*inner_pieces[s]) for s in patterns]
        operands = [mixed for _ in patterns] + [inner_pieces[s][0] for s in patterns]
        kernel = functools.partial(kernel, patterns, terms_of, tuple(range(len(inside))), inside)
        return call(
            kernel, patterns, specs + [whole_spec(x) for x in extra], operands + extra, out, scratch,
            len(patterns) * len(inside), "add_rest",
        )

    if len(last) > 2:
        core = rest(rest_kernel, last[:-2], [core], core_shape, ())
    return rest(
        last_kernel, last[-2:], [core, from_left, from_right], out_shape, (pltpu.VMEM(core_shape.shape, jnp.float32),)
    )


def solution(mesh):
    return jax.shard_map(
        shards,
        mesh=mesh,
        in_specs=(
            P(("groups", "terms"), None),
            P("groups", "terms", None),
            P(("groups", "terms"), None),
            P("groups", None),
        ),
        out_specs=P(("groups", "terms"), None),
        check_vma=False,
    )
```

```python
import functools

import jax
import jax.numpy as jnp
from jax import lax
from jax.experimental import pallas as pl
from jax.experimental.pallas import tpu as pltpu
from jax.sharding import PartitionSpec as P

REACH = 2
FIRST = 8
EARLY = ((12, "outer"), (4, "all"), (10, "outer"), (14, "outer"))
LATE = ((2, "all"), (6, "all"))


def params(megabytes=28):
    return pltpu.CompilerParams(vmem_limit_bytes=megabytes * 2**20)


def cost(pairs):
    return pl.CostEstimate(flops=pairs, bytes_accessed=pairs, transcendentals=0)


def after(x, *done):
    return lax.optimization_barrier((x, *done))[0]


def mix_kernel(chunk, left_ref, psi_ref, mixed_ref):
    terms, _, width, _ = left_ref.shape
    columns = psi_ref.shape[2]
    for t in range(0, terms, chunk):
        tall = left_ref[t : t + chunk, 0].reshape(chunk * width, width)
        product = jnp.dot(tall, psi_ref[0], preferred_element_type=jnp.float32)
        mixed_ref[t : t + chunk, 0] = product.astype(mixed_ref.dtype).reshape(chunk, width, columns)


def mix(left_env, psi):
    terms, blocks, width, _ = left_env.shape
    columns = psi.shape[2]
    inner = blocks - 2 * REACH

    def place(slot):
        return jnp.where(slot < inner, slot + REACH, jnp.where(slot < inner + REACH, slot - inner, slot))

    return pl.pallas_call(
        functools.partial(mix_kernel, 4),
        grid=(blocks,),
        in_specs=[
            pl.BlockSpec((terms, 1, width, width), lambda i: (0, place(i), 0, 0)),
            pl.BlockSpec((1, width, columns), lambda i: (place(i), 0, 0)),
        ],
        out_specs=pl.BlockSpec((terms, 1, width, columns), lambda i: (0, i, 0, 0)),
        out_shape=jax.ShapeDtypeStruct((terms, blocks, width, columns), jnp.bfloat16),
        cost_estimate=cost(terms * blocks),
        compiler_params=params(12),
        name="mix",
    )(left_env, psi)


def add_kernel(width, items, terms_of, base, finish, halos, me_ref, target_ref, *refs):
    refs = list(refs)
    mixed = [refs.pop(0) for _ in items]
    right = [refs.pop(0) for _ in items]
    before = refs.pop(0) if base else None
    from_pair, from_other = (refs.pop(0), refs.pop(0)) if halos else (None, None)
    acc = refs[-1]
    halo = REACH * width
    offset = REACH if finish in ("open", "split") else 0
    if before is None:
        acc[...] = jnp.zeros_like(acc)
    else:
        acc[...] = before[...]
    odd = me_ref[0] % 2
    if halos:
        far = acc.shape[0] - halo
        acc[pl.ds(pl.multiple_of((1 - odd) * far, halo), halo), :] += from_pair[...].astype(jnp.float32)
        acc[pl.ds(pl.multiple_of(odd * far, halo), halo), :] += from_other[...].astype(jnp.float32)
    for (s, places), m, r in zip(items, mixed, right):
        shift = target_ref[terms_of(me_ref[0], s), REACH] - REACH
        vectors = m.shape[-1] // width
        for slot, (piece, place) in enumerate(places):
            tall = jnp.concatenate(
                [m[0, slot, :, k * width : (k + 1) * width] for k in range(vectors)], axis=0
            )
            product = jnp.dot(tall, r[0, piece], preferred_element_type=jnp.float32)
            start = pl.multiple_of((place + offset + shift) * width, width)
            for k in range(vectors):
                lanes = slice(k * width, (k + 1) * width)
                acc[pl.ds(start, width), lanes] += product[k * width : (k + 1) * width]
    if finish == "split":
        own, to_pair, to_other = refs[:3]
        far = acc.shape[0] - halo
        to_pair[...] = acc[pl.ds(pl.multiple_of((1 - odd) * far, halo), halo), :].astype(to_pair.dtype)
        to_other[...] = acc[pl.ds(pl.multiple_of(odd * far, halo), halo), :].astype(to_other.dtype)
        own[...] = acc[halo:-halo]
    if finish == "final":
        refs[0][...] = acc[...].astype(refs[0].dtype)


def shards(psi, left_env, right_env, target):
    terms = target.shape[0]
    width = left_env.shape[2]
    columns = psi.shape[1]
    devices = lax.axis_size("terms")
    stride = devices // terms
    blocks = psi.shape[0] // width
    per_class = blocks // stride
    me = lax.axis_index("terms")
    me_ref = me.astype(jnp.int32).reshape(1)
    spans = {
        "all": ((0, blocks),),
        "outer": ((0, REACH), (blocks - REACH, blocks)),
        "inner": ((REACH, blocks - REACH),),
    }
    by_partner = stride == 1 and terms == 16
    terms_of = (lambda own, s: jnp.bitwise_xor(own, s)) if by_partner else (lambda own, s: s)
    halo = REACH * width
    open_shape = jax.ShapeDtypeStruct((blocks * width + 2 * halo, columns), jnp.float32)
    core_shape = jax.ShapeDtypeStruct((blocks * width, columns), jnp.float32)
    halo_shape = jax.ShapeDtypeStruct((halo, columns), jnp.bfloat16)
    out_shape = jax.ShapeDtypeStruct((blocks * width, columns), jnp.bfloat16)

    psi_blocks = psi.reshape(blocks, width, columns)
    left_blocks = left_env.reshape(terms, blocks, width, width)
    right = right_env.reshape(devices, per_class, width, width)

    def whole(x):
        return pl.BlockSpec(x.shape, lambda i, me, target, nd=len(x.shape): (0,) * nd)

    def add(mixed, pieces, before, finish, halos=()):
        items, specs = [], []
        for s, kind, array, at in pieces:
            held = [place for a, b in spans[kind] for place in range(a, b)]
            by_slot = held if kind != "all" else held[REACH:-REACH] + held[:REACH] + held[-REACH:]
            items.append((s, tuple((held.index(place), place) for place in by_slot)))
            specs.append(
                pl.BlockSpec(
                    (1, len(held), width, columns),
                    lambda i, me, target, s=s, slot=int(kind == "outer"): (terms_of(me[0], s), slot, 0, 0),
                )
            )
        for s, kind, array, at in pieces:
            where = at if callable(at) else (lambda own, at=at: at)
            specs.append(
                pl.BlockSpec((1, *array.shape[1:]), lambda i, me, target, where=where: (where(me[0]), 0, 0, 0))
            )
        extra = [*([] if before is None else [before]), *halos]
        outs = {
            "open": (open_shape,),
            "split": (core_shape, halo_shape, halo_shape),
            "core": (core_shape,),
            "final": (out_shape,),
        }[finish]
        scratch = {"split": open_shape, "final": core_shape}.get(finish)
        got = pl.pallas_call(
            functools.partial(add_kernel, width, tuple(items), terms_of, before is not None, finish, bool(halos)),
            grid_spec=pltpu.PrefetchScalarGridSpec(
                num_scalar_prefetch=2,
                grid=(1,),
                in_specs=specs + [whole(x) for x in extra],
                out_specs=tuple(whole(x) for x in outs),
                scratch_shapes=[] if scratch is None else [pltpu.VMEM(scratch.shape, scratch.dtype)],
            ),
            out_shape=outs,
            cost_estimate=cost(len(pieces) * blocks),
            compiler_params=params(),
            name="add_" + finish,
        )(me_ref, target, *[mixed for _ in pieces], *[p[2] for p in pieces], *extra)
        return got if len(outs) > 1 else got[0]

    def neighbours(to_pair, to_other):
        from_pair = lax.ppermute(to_pair, "terms", [(i, i ^ 1) for i in range(devices)])
        others = [(i, i + 1) for i in range(1, devices - 1, 2)]
        from_other = lax.ppermute(to_other, "terms", others + [(b, a) for a, b in others])
        return from_pair, from_other

    if not by_partner:
        got = lax.all_to_all(right, "terms", split_axis=0, concat_axis=0, tiled=True)
        got = got.reshape(terms, stride, per_class, width, width)
        got = jnp.swapaxes(got, 1, 2).reshape(terms, blocks, width, width)
        mixed = mix(left_blocks, psi_blocks)
        sums = None
        step = max(1, terms // 4)
        for a in range(0, terms - step, step):
            sums = add(mixed, [(s, "all", got, s) for s in range(a, a + step)], sums, "open")
        core, to_pair, to_other = add(mixed, [(s, "all", got, s) for s in range(a + step, terms)], sums, "split")
        return add(mixed, [], core, "final", neighbours(to_pair, to_other))

    def move(operand, s):
        return lax.ppermute(operand, "terms", [(i, i ^ s) for i in range(devices)])

    def pick(source, index, start, count):
        return lax.dynamic_slice(source, (index, start, 0, 0), (1, count, width, width))

    arrived = {}

    def send(source, relayed, s, kind):
        partner = jnp.bitwise_xor(me, s)
        parts = [
            jnp.concatenate([pick(array, partner, a, b - a) for a, b in spans[kind]], axis=1)
            for array in (source, relayed)
        ]
        message = jnp.concatenate(parts, axis=0)
        got = move(message, s)
        arrived[s, kind], arrived[s + 1, kind] = (got, 0), (got, 1)
        return message

    def send_single(source, s, kind, term):
        partner = jnp.bitwise_xor(me, s)
        message = jnp.concatenate([pick(source, partner, a, b - a) for a, b in spans[kind]], axis=1)
        arrived[term, kind] = (move(message, s), 0)

    def items(*keys):
        return [(s, kind, *arrived[s, kind]) for s, kind in keys]

    def pairs(messages):
        return [(t, kind) for s, kind in messages for t in (s, s + 1)]

    exchanged = move(right, 1)
    first = pick(right, jnp.bitwise_xor(me, FIRST), 0, blocks)
    arrived[0, "all"] = (right, lambda own: own)
    arrived[1, "all"] = (exchanged, lambda own: own)
    arrived[FIRST, "all"] = (move(first, FIRST), 0)
    messages = [first]
    for s, kind in EARLY:
        messages.append(send(after(right, messages[-1]), after(exchanged, messages[-1]), s, kind))
    mixed = mix(after(left_blocks, *messages), psi_blocks)
    source, relayed = after(right, mixed), after(exchanged, mixed)
    send_single(relayed, FIRST, "all", FIRST + 1)
    send(source, relayed, *LATE[1])
    sums = add(mixed, items((0, "all"), (1, "all"), (FIRST, "all"), *pairs(EARLY[:1])), None, "open")
    source, relayed = after(right, sums), after(exchanged, sums)
    send(source, relayed, *LATE[0])
    send(source, relayed, 12, "inner")
    send(source, relayed, 10, "inner")
    send_single(source, 14, "inner", 14)
    send_single(relayed, 14, "inner", 15)
    sums = add(mixed, items(*pairs(EARLY[1:3])), sums, "open")
    core, to_pair, to_other = add(mixed, items((FIRST + 1, "all"), *pairs(EARLY[3:] + LATE)), sums, "split")
    halos = neighbours(to_pair, to_other)
    core = add(mixed, items(*pairs([(12, "inner")])), core, "core")
    core = add(mixed, items(*pairs([(10, "inner")])), core, "core", halos)
    return add(mixed, items(*pairs([(14, "inner")])), core, "final")


def solution(mesh):
    return jax.shard_map(
        shards,
        mesh=mesh,
        in_specs=(
            P(("groups", "terms"), None),
            P("groups", "terms", None),
            P(("groups", "terms"), None),
            P("groups", None),
        ),
        out_specs=P(("groups", "terms"), None),
        check_vma=False,
    )
```

```python
import functools

import jax
import jax.numpy as jnp
from jax import lax
from jax.experimental import pallas as pl
from jax.experimental.pallas import tpu as pltpu
from jax.sharding import PartitionSpec as P

REACH = 2
FIRST = 8
EARLY = ((12, "outer"), (6, "all"), (10, "outer"), (14, "outer"))
LATE = ((2, "all"), (4, "all"))


def params(megabytes=28):
    return pltpu.CompilerParams(vmem_limit_bytes=megabytes * 2**20)


def cost(pairs):
    return pl.CostEstimate(flops=pairs, bytes_accessed=pairs, transcendentals=0)


def after(x, *done):
    return lax.optimization_barrier((x, *done))[0]


def mix_kernel(chunk, left_ref, psi_ref, mixed_ref):
    terms, _, width, _ = left_ref.shape
    columns = psi_ref.shape[2]
    for t in range(0, terms, chunk):
        tall = left_ref[t : t + chunk, 0].reshape(chunk * width, width)
        product = jnp.dot(tall, psi_ref[0], preferred_element_type=jnp.float32)
        mixed_ref[t : t + chunk, 0] = product.astype(mixed_ref.dtype).reshape(chunk, width, columns)


def mix(left_env, psi):
    terms, blocks, width, _ = left_env.shape
    columns = psi.shape[2]
    inner = blocks - 2 * REACH

    def place(slot):
        return jnp.where(slot < inner, slot + REACH, jnp.where(slot < inner + REACH, slot - inner, slot))

    return pl.pallas_call(
        functools.partial(mix_kernel, min(4, terms)),
        grid=(blocks,),
        in_specs=[
            pl.BlockSpec((terms, 1, width, width), lambda i: (0, place(i), 0, 0)),
            pl.BlockSpec((1, width, columns), lambda i: (place(i), 0, 0)),
        ],
        out_specs=pl.BlockSpec((terms, 1, width, columns), lambda i: (0, i, 0, 0)),
        out_shape=jax.ShapeDtypeStruct((terms, blocks, width, columns), jnp.bfloat16),
        cost_estimate=cost(terms * blocks),
        compiler_params=params(12),
        name="mix",
    )(left_env, psi)


def add_kernel(width, items, terms_of, base, finish, halos, me_ref, target_ref, *refs):
    refs = list(refs)
    mixed = [refs.pop(0) for _ in items]
    right = [refs.pop(0) for _ in items]
    before = refs.pop(0) if base else None
    came = [refs.pop(0) for _ in halos]
    acc = refs[-1]
    halo = REACH * width
    offset = REACH if finish in ("open", "split") else 0
    if before is None:
        acc[...] = jnp.zeros_like(acc)
    else:
        acc[...] = before[...]
    odd = me_ref[0] % 2
    for kind, array in zip(halos, came):
        far = acc.shape[0] - halo
        side = 1 - odd if kind == "pair" else odd
        acc[pl.ds(pl.multiple_of(side * far, halo), halo), :] += array[...].astype(jnp.float32)
    for (s, places), m, r in zip(items, mixed, right):
        shift = target_ref[terms_of(me_ref[0], s), REACH] - REACH
        vectors = m.shape[-1] // width
        for slot, (piece, place) in enumerate(places):
            tall = jnp.concatenate(
                [m[0, slot, :, k * width : (k + 1) * width] for k in range(vectors)], axis=0
            )
            product = jnp.dot(tall, r[0, piece], preferred_element_type=jnp.float32)
            start = pl.multiple_of((place + offset + shift) * width, width)
            for k in range(vectors):
                lanes = slice(k * width, (k + 1) * width)
                acc[pl.ds(start, width), lanes] += product[k * width : (k + 1) * width]
    if finish == "split":
        own, to_pair, to_other = refs[:3]
        far = acc.shape[0] - halo
        to_pair[...] = acc[pl.ds(pl.multiple_of((1 - odd) * far, halo), halo), :].astype(to_pair.dtype)
        to_other[...] = acc[pl.ds(pl.multiple_of(odd * far, halo), halo), :].astype(to_other.dtype)
        own[...] = acc[halo:-halo]
    if finish == "final":
        refs[0][...] = acc[...].astype(refs[0].dtype)


def shards(psi, left_env, right_env, target):
    terms = target.shape[0]
    width = left_env.shape[2]
    columns = psi.shape[1]
    devices = lax.axis_size("terms")
    stride = devices // terms
    blocks = psi.shape[0] // width
    per_class = blocks // stride
    me = lax.axis_index("terms")
    me_ref = me.astype(jnp.int32).reshape(1)
    spans = {
        "all": ((0, blocks),),
        "outer": ((0, REACH), (blocks - REACH, blocks)),
        "inner": ((REACH, blocks - REACH),),
    }
    by_partner = stride == 1 and terms == 16
    terms_of = (lambda own, s: jnp.bitwise_xor(own, s)) if by_partner else (lambda own, s: s)
    halo = REACH * width
    open_shape = jax.ShapeDtypeStruct((blocks * width + 2 * halo, columns), jnp.float32)
    core_shape = jax.ShapeDtypeStruct((blocks * width, columns), jnp.float32)
    halo_shape = jax.ShapeDtypeStruct((halo, columns), jnp.bfloat16)
    out_shape = jax.ShapeDtypeStruct((blocks * width, columns), jnp.bfloat16)

    psi_blocks = psi.reshape(blocks, width, columns)
    left_blocks = left_env.reshape(terms, blocks, width, width)
    right = right_env.reshape(devices, per_class, width, width)

    def whole(x):
        return pl.BlockSpec(x.shape, lambda i, me, target, nd=len(x.shape): (0,) * nd)

    def add(mixed, pieces, before, finish, halos=()):
        items, specs = [], []
        for s, kind, array, at in pieces:
            held = [place for a, b in spans[kind] for place in range(a, b)]
            by_slot = held if kind != "all" else held[REACH:-REACH] + held[:REACH] + held[-REACH:]
            items.append((s, tuple((held.index(place), place) for place in by_slot)))
            specs.append(
                pl.BlockSpec(
                    (1, len(held), width, columns),
                    lambda i, me, target, s=s, slot=int(kind == "outer"): (terms_of(me[0], s), slot, 0, 0),
                )
            )
        for s, kind, array, at in pieces:
            where = at if callable(at) else (lambda own, at=at: at)
            specs.append(
                pl.BlockSpec((1, *array.shape[1:]), lambda i, me, target, where=where: (where(me[0]), 0, 0, 0))
            )
        extra = [*([] if before is None else [before]), *(array for _, array in halos)]
        outs = {
            "open": (open_shape,),
            "split": (core_shape, halo_shape, halo_shape),
            "core": (core_shape,),
            "final": (out_shape,),
        }[finish]
        scratch = {"split": open_shape, "final": core_shape}.get(finish)
        got = pl.pallas_call(
            functools.partial(add_kernel, width, tuple(items), terms_of, before is not None, finish, tuple(kind for kind, _ in halos)),
            grid_spec=pltpu.PrefetchScalarGridSpec(
                num_scalar_prefetch=2,
                grid=(1,),
                in_specs=specs + [whole(x) for x in extra],
                out_specs=tuple(whole(x) for x in outs),
                scratch_shapes=[] if scratch is None else [pltpu.VMEM(scratch.shape, scratch.dtype)],
            ),
            out_shape=outs,
            cost_estimate=cost(len(pieces) * blocks),
            compiler_params=params(),
            name="add_" + finish,
        )(me_ref, target, *[mixed for _ in pieces], *[p[2] for p in pieces], *extra)
        return got if len(outs) > 1 else got[0]

    def neighbours(to_pair, to_other):
        from_pair = lax.ppermute(to_pair, "terms", [(i, i ^ 1) for i in range(devices)])
        others = [(i, i + 1) for i in range(1, devices - 1, 2)]
        from_other = lax.ppermute(to_other, "terms", others + [(b, a) for a, b in others])
        return ("pair", from_pair), ("other", from_other)

    if not by_partner:
        got = lax.all_to_all(right, "terms", split_axis=0, concat_axis=0, tiled=True)
        got = got.reshape(terms, stride, per_class, width, width)
        got = jnp.swapaxes(got, 1, 2).reshape(terms, blocks, width, width)
        mixed = mix(left_blocks, psi_blocks)
        sums = None
        step = max(1, terms // 4)
        for a in range(0, terms - step, step):
            sums = add(mixed, [(s, "all", got, s) for s in range(a, a + step)], sums, "open")
        core, to_pair, to_other = add(mixed, [(s, "all", got, s) for s in range(a + step, terms)], sums, "split")
        return add(mixed, [], core, "final", neighbours(to_pair, to_other))

    def move(operand, s):
        return lax.ppermute(operand, "terms", [(i, i ^ s) for i in range(devices)])

    def pick(source, index, start, count):
        return lax.dynamic_slice(source, (index, start, 0, 0), (1, count, width, width))

    arrived = {}

    def send(source, relayed, s, kind):
        partner = jnp.bitwise_xor(me, s)
        parts = [
            jnp.concatenate([pick(array, partner, a, b - a) for a, b in spans[kind]], axis=1)
            for array in (source, relayed)
        ]
        message = jnp.concatenate(parts, axis=0)
        got = move(message, s)
        arrived[s, kind], arrived[s + 1, kind] = (got, 0), (got, 1)
        return message

    def send_single(source, s, kind, term):
        partner = jnp.bitwise_xor(me, s)
        message = jnp.concatenate([pick(source, partner, a, b - a) for a, b in spans[kind]], axis=1)
        arrived[term, kind] = (move(message, s), 0)

    def items(*keys):
        return [(s, kind, *arrived[s, kind]) for s, kind in keys]

    def pairs(messages):
        return [(t, kind) for s, kind in messages for t in (s, s + 1)]

    exchanged = move(right, 1)
    first = pick(right, jnp.bitwise_xor(me, FIRST), 0, blocks)
    arrived[0, "all"] = (right, lambda own: own)
    arrived[1, "all"] = (exchanged, lambda own: own)
    arrived[FIRST, "all"] = (move(first, FIRST), 0)
    messages = [first]
    for s, kind in EARLY:
        messages.append(send(after(right, messages[-1]), after(exchanged, messages[-1]), s, kind))
    mixed = mix(after(left_blocks, *messages), psi_blocks)
    source, relayed = after(right, mixed), after(exchanged, mixed)
    send_single(relayed, FIRST, "all", FIRST + 1)
    send(source, relayed, *LATE[1])
    sums = add(mixed, items((0, "all"), (1, "all"), (FIRST, "all"), *pairs(EARLY[:1])), None, "open")
    source, relayed = after(right, sums), after(exchanged, sums)
    send(source, relayed, *LATE[0])
    send(source, relayed, 12, "inner")
    send(source, relayed, 10, "inner")
    send_single(source, 14, "inner", 14)
    send_single(relayed, 14, "inner", 15)
    sums = add(mixed, items(*pairs(EARLY[1:3])), sums, "open")
    core, to_pair, to_other = add(mixed, items((FIRST + 1, "all"), *pairs(EARLY[3:] + LATE)), sums, "split")
    halos = neighbours(to_pair, to_other)
    core = add(mixed, [], core, "core", halos[:1])
    core = add(mixed, items(*pairs([(12, "inner"), (10, "inner")])), core, "core", halos[1:])
    return add(mixed, items(*pairs([(14, "inner")])), core, "final")


def solution(mesh):
    return jax.shard_map(
        shards,
        mesh=mesh,
        in_specs=(
            P(("groups", "terms"), None),
            P("groups", "terms", None),
            P(("groups", "terms"), None),
            P("groups", None),
        ),
        out_specs=P(("groups", "terms"), None),
        check_vma=False,
    )
```

```python
import functools

import jax
import jax.numpy as jnp
from jax import lax
from jax.experimental import pallas as pl
from jax.experimental.pallas import tpu as pltpu
from jax.sharding import PartitionSpec as P

REACH = 2
FIRST = 8
EARLY = ((12, "outer"), (6, "all"), (10, "outer"), (14, "outer"))
LATE = ((2, "all"), (4, "all"))


def params(megabytes=28):
    return pltpu.CompilerParams(vmem_limit_bytes=megabytes * 2**20)


def cost(pairs):
    return pl.CostEstimate(flops=pairs, bytes_accessed=pairs, transcendentals=0)


def after(x, *done):
    return lax.optimization_barrier((x, *done))[0]


def mix_kernel(chunk, left_ref, psi_ref, mixed_ref):
    terms, _, width, _ = left_ref.shape
    columns = psi_ref.shape[2]
    for t in range(0, terms, chunk):
        tall = left_ref[t : t + chunk, 0].reshape(chunk * width, width)
        product = jnp.dot(tall, psi_ref[0], preferred_element_type=jnp.float32)
        mixed_ref[t : t + chunk, 0] = product.astype(mixed_ref.dtype).reshape(chunk, width, columns)


def mix(left_env, psi):
    terms, blocks, width, _ = left_env.shape
    columns = psi.shape[2]
    inner = blocks - 2 * REACH

    def place(slot):
        return jnp.where(slot < inner, slot + REACH, jnp.where(slot < inner + REACH, slot - inner, slot))

    return pl.pallas_call(
        functools.partial(mix_kernel, min(4, terms)),
        grid=(blocks,),
        in_specs=[
            pl.BlockSpec((terms, 1, width, width), lambda i: (0, place(i), 0, 0)),
            pl.BlockSpec((1, width, columns), lambda i: (place(i), 0, 0)),
        ],
        out_specs=pl.BlockSpec((terms, 1, width, columns), lambda i: (0, i, 0, 0)),
        out_shape=jax.ShapeDtypeStruct((terms, blocks, width, columns), jnp.bfloat16),
        cost_estimate=cost(terms * blocks),
        compiler_params=params(12),
        name="mix",
    )(left_env, psi)


def add_kernel(width, items, terms_of, base, finish, halos, me_ref, target_ref, *refs):
    refs = list(refs)
    mixed = [refs.pop(0) for _ in items]
    right = [refs.pop(0) for _ in items]
    before = refs.pop(0) if base else None
    came = [refs.pop(0) for _ in halos]
    acc = refs[-1]
    halo = REACH * width
    offset = REACH if finish in ("open", "split") else 0
    if before is None:
        acc[...] = jnp.zeros_like(acc)
    else:
        acc[...] = before[...]
    odd = me_ref[0] % 2
    for kind, array in zip(halos, came):
        far = acc.shape[0] - halo
        side = 1 - odd if kind == "pair" else odd
        acc[pl.ds(pl.multiple_of(side * far, halo), halo), :] += array[...].astype(jnp.float32)
    for (s, places), m, r in zip(items, mixed, right):
        shift = target_ref[terms_of(me_ref[0], s), REACH] - REACH
        vectors = m.shape[-1] // width
        for slot, (piece, place) in enumerate(places):
            tall = jnp.concatenate(
                [m[0, slot, :, k * width : (k + 1) * width] for k in range(vectors)], axis=0
            )
            product = jnp.dot(tall, r[0, piece], preferred_element_type=jnp.float32)
            start = pl.multiple_of((place + offset + shift) * width, width)
            for k in range(vectors):
                lanes = slice(k * width, (k + 1) * width)
                acc[pl.ds(start, width), lanes] += product[k * width : (k + 1) * width]
    if finish == "split":
        own, to_pair, to_other = refs[:3]
        far = acc.shape[0] - halo
        to_pair[...] = acc[pl.ds(pl.multiple_of((1 - odd) * far, halo), halo), :].astype(to_pair.dtype)
        to_other[...] = acc[pl.ds(pl.multiple_of(odd * far, halo), halo), :].astype(to_other.dtype)
        own[...] = acc[halo:-halo]
    if finish == "final":
        refs[0][...] = acc[...].astype(refs[0].dtype)


def shards(psi, left_env, right_env, target):
    terms = target.shape[0]
    width = left_env.shape[2]
    columns = psi.shape[1]
    devices = lax.axis_size("terms")
    stride = devices // terms
    blocks = psi.shape[0] // width
    per_class = blocks // stride
    me = lax.axis_index("terms")
    me_ref = me.astype(jnp.int32).reshape(1)
    spans = {
        "all": ((0, blocks),),
        "outer": ((0, REACH), (blocks - REACH, blocks)),
        "inner": ((REACH, blocks - REACH),),
    }
    by_partner = stride == 1 and terms == 16
    terms_of = (lambda own, s: jnp.bitwise_xor(own, s)) if by_partner else (lambda own, s: s)
    halo = REACH * width
    open_shape = jax.ShapeDtypeStruct((blocks * width + 2 * halo, columns), jnp.float32)
    core_shape = jax.ShapeDtypeStruct((blocks * width, columns), jnp.float32)
    halo_shape = jax.ShapeDtypeStruct((halo, columns), jnp.bfloat16)
    out_shape = jax.ShapeDtypeStruct((blocks * width, columns), jnp.bfloat16)

    psi_blocks = psi.reshape(blocks, width, columns)
    left_blocks = left_env.reshape(terms, blocks, width, width)
    right = right_env.reshape(devices, per_class, width, width)

    def whole(x):
        return pl.BlockSpec(x.shape, lambda i, me, target, nd=len(x.shape): (0,) * nd)

    def add(mixed, pieces, before, finish, halos=()):
        items, specs = [], []
        for s, kind, array, at in pieces:
            held = [place for a, b in spans[kind] for place in range(a, b)]
            by_slot = held if kind != "all" else held[REACH:-REACH] + held[:REACH] + held[-REACH:]
            items.append((s, tuple((held.index(place), place) for place in by_slot)))
            specs.append(
                pl.BlockSpec(
                    (1, len(held), width, columns),
                    lambda i, me, target, s=s, slot=int(kind == "outer"): (terms_of(me[0], s), slot, 0, 0),
                )
            )
        for s, kind, array, at in pieces:
            where = at if callable(at) else (lambda own, at=at: at)
            specs.append(
                pl.BlockSpec((1, *array.shape[1:]), lambda i, me, target, where=where: (where(me[0]), 0, 0, 0))
            )
        extra = [*([] if before is None else [before]), *(array for _, array in halos)]
        outs = {
            "open": (open_shape,),
            "split": (core_shape, halo_shape, halo_shape),
            "core": (core_shape,),
            "final": (out_shape,),
        }[finish]
        scratch = {"split": open_shape, "final": core_shape}.get(finish)
        got = pl.pallas_call(
            functools.partial(add_kernel, width, tuple(items), terms_of, before is not None, finish, tuple(kind for kind, _ in halos)),
            grid_spec=pltpu.PrefetchScalarGridSpec(
                num_scalar_prefetch=2,
                grid=(1,),
                in_specs=specs + [whole(x) for x in extra],
                out_specs=tuple(whole(x) for x in outs),
                scratch_shapes=[] if scratch is None else [pltpu.VMEM(scratch.shape, scratch.dtype)],
            ),
            out_shape=outs,
            cost_estimate=cost(len(pieces) * blocks),
            compiler_params=params(),
            name="add_" + finish,
        )(me_ref, target, *[mixed for _ in pieces], *[p[2] for p in pieces], *extra)
        return got if len(outs) > 1 else got[0]

    def neighbours(to_pair, to_other):
        from_pair = lax.ppermute(to_pair, "terms", [(i, i ^ 1) for i in range(devices)])
        others = [(i, i + 1) for i in range(1, devices - 1, 2)]
        from_other = lax.ppermute(to_other, "terms", others + [(b, a) for a, b in others])
        return ("pair", from_pair), ("other", from_other)

    if not by_partner:
        got = lax.all_to_all(right, "terms", split_axis=0, concat_axis=0, tiled=True)
        got = got.reshape(terms, stride, per_class, width, width)
        got = jnp.swapaxes(got, 1, 2).reshape(terms, blocks, width, width)
        mixed = mix(left_blocks, psi_blocks)
        sums = None
        step = max(1, terms // 4)
        for a in range(0, terms - step, step):
            sums = add(mixed, [(s, "all", got, s) for s in range(a, a + step)], sums, "open")
        core, to_pair, to_other = add(mixed, [(s, "all", got, s) for s in range(a + step, terms)], sums, "split")
        return add(mixed, [], core, "final", neighbours(to_pair, to_other))

    def move(operand, s):
        return lax.ppermute(operand, "terms", [(i, i ^ s) for i in range(devices)])

    def pick(source, index, start, count):
        return lax.dynamic_slice(source, (index, start, 0, 0), (1, count, width, width))

    arrived = {}

    def send(source, relayed, s, kind):
        partner = jnp.bitwise_xor(me, s)
        parts = [
            jnp.concatenate([pick(array, partner, a, b - a) for a, b in spans[kind]], axis=1)
            for array in (source, relayed)
        ]
        message = jnp.concatenate(parts, axis=0)
        got = move(message, s)
        arrived[s, kind], arrived[s + 1, kind] = (got, 0), (got, 1)
        return message

    def send_single(source, s, kind, term):
        partner = jnp.bitwise_xor(me, s)
        message = jnp.concatenate([pick(source, partner, a, b - a) for a, b in spans[kind]], axis=1)
        arrived[term, kind] = (move(message, s), 0)

    def items(*keys):
        return [(s, kind, *arrived[s, kind]) for s, kind in keys]

    def pairs(messages):
        return [(t, kind) for s, kind in messages for t in (s, s + 1)]

    exchanged = move(right, 1)
    first = pick(right, jnp.bitwise_xor(me, FIRST), 0, blocks)
    arrived[0, "all"] = (right, lambda own: own)
    arrived[1, "all"] = (exchanged, lambda own: own)
    arrived[FIRST, "all"] = (move(first, FIRST), 0)
    messages = [first]
    for s, kind in EARLY:
        messages.append(send(after(right, messages[-1]), after(exchanged, messages[-1]), s, kind))
    mixed = mix(after(left_blocks, *messages), psi_blocks)
    source, relayed = after(right, mixed), after(exchanged, mixed)
    send_single(relayed, FIRST, "all", FIRST + 1)
    send(source, relayed, *LATE[1])
    sums = add(mixed, items((0, "all"), (1, "all"), (FIRST, "all"), *pairs(EARLY[:1])), None, "open")
    source, relayed = after(right, sums), after(exchanged, sums)
    send(source, relayed, *LATE[0])
    send(source, relayed, 10, "inner")
    send(source, relayed, 14, "inner")
    send_single(source, 12, "inner", 12)
    send_single(relayed, 12, "inner", 13)
    sums = add(mixed, items(*pairs(EARLY[1:3])), sums, "open")
    core, to_pair, to_other = add(mixed, items((FIRST + 1, "all"), *pairs(EARLY[3:] + LATE)), sums, "split")
    halos = neighbours(to_pair, to_other)
    core = add(mixed, [], core, "core", halos[:1])
    core = add(mixed, items(*pairs([(10, "inner"), (14, "inner")])), core, "core", halos[1:])
    return add(mixed, items(*pairs([(12, "inner")])), core, "final")


def solution(mesh):
    return jax.shard_map(
        shards,
        mesh=mesh,
        in_specs=(
            P(("groups", "terms"), None),
            P("groups", "terms", None),
            P(("groups", "terms"), None),
            P("groups", None),
        ),
        out_specs=P(("groups", "terms"), None),
        check_vma=False,
    )
```
